256 devices in a mesh: expert: 64 (over x, z, core), et: 4 (over y).
Axes of the slice: x: 4, y: 4, z: 8, core: 2. Of those that a mesh axis runs over, the one named last changes fastest.
Arguments:
- grad_out: bfloat16 [8192, 3584], P('expert', 'et'), may hold values from -0.59765625 to 0.59765625
- routing: int32 [8192, 8], P('expert'), may hold values from 0 to 127, all different within a row; in each aligned block of 128 rows (0 to 127, 128 to 255, ...) at most 16 rows name the same one
- gates: float32 [8192, 8], P('expert'), may hold values from 0.1 to 1
- hidden: bfloat16 [128, 1024, 1024], P('expert', None, 'et'), may hold values from -42 to 42, as said below
- momentum: bfloat16 [128, 3584, 1024], P('expert', None, 'et'), may hold values from -6 to 6
- right_factor: float32 [128, 32, 1024], P('expert', None, 'et'), may hold values from -0.1875 to 0.1875
Outputs:
- new_momentum: bfloat16 [128, 3584, 1024], P('expert', None, 'et')
- left_factor: float32 [128, 32, 3584], P('expert')
- new_right: float32 [128, 32, 1024], P('expert', None, 'et')
The draws below stay inside these ranges and needn't reach their ends.
Inputs may be any that keep to these rules, and one draw needn't show every extreme that they name: `routing`: each row names 8 different experts; among the 128 rows of one index of expert no expert is named more than 16 times, a bound that some block reaches. `hidden`: slots that no token fills hold arbitrary values.
All inputs are finite; a program needn't handle non-finite values.
Results may differ from the reference program's by a relative error of at most 0.0048.
Values may be sent and summed in bfloat16 or wider, within the bound.
No kernel may reach another device: no remote copies, remote signals or barrier semaphores. Data moves between devices by JAX's collectives and lax.ppermute only.
A program may use at most 128 MiB of HBM per device.

```python
import math
import jax
import jax.numpy as jnp
import numpy as np
from jax import lax

D = 3584
H = 1024
TOPK = 8
R = 32
TOK_DEV = 128
EXPERTS = 128
TOKENS = 8192
CAP = 16
SLOTS = 1024
N_EXPERT = 64


def draw_hidden(key, part):
    key = jax.random.fold_in(key, 11)
    first, second = jax.random.split(key, 2)
    ramp = jnp.arange(H, dtype=jnp.float32) / H
    column_scale = jnp.exp(jax.random.uniform(second, (H,), jnp.float32, 0.0, math.log(10.0))) * jnp.exp(math.log(3.0) * ramp) / 5.0
    entries = jnp.clip(jax.random.normal(first, (EXPERTS, SLOTS, H), jnp.float32), -4.0, 4.0)
    values = entries * column_scale[None, None, :]
    return values.astype(jnp.bfloat16)


def steps_of(own_key, shape, pieces, least, top_value):
    def one(axis_at, parts):
        steps = jax.random.uniform(jax.random.fold_in(jax.random.fold_in(own_key, 6), axis_at), (parts,), jnp.float32, least / len(pieces), top_value / len(pieces))
        return jnp.repeat(jnp.exp(steps), shape[axis_at] // parts).reshape((-1,) + (1,) * (len(shape) - axis_at - 1))

    loudness = one(*pieces[0])
    for cut in pieces[1:]:
        loudness = loudness * one(*cut)
    return loudness


def assign_block(key, own, number, rows, number_of, top, reach, skew):
    order = jax.random.permutation(key, number_of)
    heavy_load, ordinary = load_shares(number_of, rows * top, reach, skew, True), load_shares(number_of, rows * top, reach, skew, False)
    places = jnp.arange(number_of)

    def named(sizes, offset_by):
        used = int((sizes > 0).sum())
        fixed = max(1, used // 4)
        passed = fixed + (places - fixed + offset_by * (used - fixed)) % max(1, number_of - fixed)
        return jnp.zeros((number_of,), jnp.int32).at[order[jnp.where(places < fixed, places, passed)]].set(jnp.asarray(sizes, jnp.int32))

    sizes = jnp.where(number % 4 == 0, named(heavy_load, number // 4), named(ordinary, number - number // 4 - 1))
    mixed = jax.random.permutation(jax.random.fold_in(own, 3), number_of)
    giver, sink = mixed[0:number_of // 2 * 2:2], mixed[1:number_of // 2 * 2:2]
    room = jnp.minimum(sizes[giver] - 1, reach - sizes[sink]) // 2
    room = jnp.where((giver == order[0]) | (sink == order[0]) | (sizes[sink] == 0), 0, jnp.maximum(room, 0))
    passed = jax.random.randint(jax.random.fold_in(own, 4), (number_of // 2,), 0, 1 << 20) % (room + 1)
    sizes = sizes.at[giver].add(-passed).at[sink].add(passed)
    items = jnp.searchsorted(jnp.cumsum(sizes), jnp.arange(rows * top), side="right").astype(jnp.int32)
    grid = items.reshape(top, rows).T
    grid = grid[jax.random.permutation(jax.random.fold_in(own, 1), rows)]
    offset_by = jax.random.randint(jax.random.fold_in(own, 2), (rows, 1), 0, top)
    return jnp.take_along_axis(grid, (jnp.arange(top)[None, :] + offset_by) % top, axis=1)


def load_shares(number_of, total, reach, skew, full):
    loads = [(1 << 20) // math.isqrt(grade ** skew) + 1 for grade in range(1, number_of + 1)]
    largest = reach if full else min(reach, max(-(-total // number_of), total * loads[0] // sum(loads)))
    least = 1 if total - largest >= number_of - 1 else 0
    holding, spare = [largest] + [least] * (number_of - 1), total - largest - least * (number_of - 1)
    while spare > 0:
        movable = [i for i in range(1, number_of) if holding[i] < largest] or [i for i in range(1, number_of) if holding[i] < reach]
        mass, budget = sum([loads[i] for i in movable]), spare
        for i in movable:
            more = min(reach - holding[i], max(1, budget * loads[i] // mass), spare)
            holding[i] = holding[i] + more
            spare = spare - more
    return np.array(holding)


def bell_draw(own_key, extent, scale, bound, shards=(), held_as=jnp.bfloat16):
    result = jax.random.normal(own_key, extent, jnp.float32) * scale
    if len(shards) > 0:
        result = steps_of(own_key, extent, shards, -0.22, 0.18) * result
    return jnp.clip(result, min=-bound, max=bound).astype(held_as)


def setup_inputs(seed: int = 0) -> dict:
    splits = jax.random.split(jax.random.key(seed), 7)
    grad_out = bell_draw(splits[0], (TOKENS, D), 0.1, 0.59765625, ((0, 64), (1, 4)))
    routing_keys = jax.random.split(jax.random.fold_in(splits[1], 1), TOKENS // TOK_DEV)
    routing_turns = jax.random.permutation(jax.random.fold_in(splits[1], 3), TOKENS // TOK_DEV)
    routing = jax.vmap(lambda own, number: assign_block(jax.random.fold_in(splits[1], 2), own, number, TOK_DEV, EXPERTS, TOPK, CAP, 2))(routing_keys, routing_turns).reshape((TOKENS, TOPK))
    gates = jnp.clip(0.1 + 0.9 * jax.random.uniform(splits[2], (TOKENS, TOPK), jnp.float32) ** steps_of(splits[2], (TOKENS, TOPK), ((0, 64),), -0.2, 0.2), 0.1, 1.0)
    hidden = draw_hidden(jax.random.fold_in(splits[6], 71), 0)
    momentum = bell_draw(splits[4], (EXPERTS, D, H), 1.0, 6.0, ((0, 64), (2, 4)))
    right_factor = bell_draw(splits[5], (EXPERTS, R, H), H ** -0.5, 0.1875, ((0, 64), (2, 4)), jnp.float32)
    return dict(grad_out=grad_out, routing=routing, gates=gates, hidden=hidden, momentum=momentum, right_factor=right_factor)


momentum_decay = 0.95
epsilon = 1e-06

def slot_table(routing):
    routes_flat = routing.reshape(N_EXPERT, TOK_DEV * TOPK)
    expert_ids = jnp.arange(EXPERTS, dtype=jnp.int32)
    one_hot = (routes_flat[:, :, None] == expert_ids[None, None, :]).astype(jnp.int32)
    before = jnp.cumsum(one_hot, axis=1) - one_hot
    slot_index = lax.optimization_barrier(jnp.sum(before * one_hot, axis=2)).astype(jnp.int32)
    source = jnp.arange(N_EXPERT, dtype=jnp.int32)[:, None]
    target = (routes_flat * SLOTS + source * CAP + slot_index).astype(jnp.int32)
    owner_table = jnp.full((EXPERTS * SLOTS,), -1, dtype=jnp.int32)
    owner_table = owner_table.at[target.reshape(-1)].set(jnp.arange(TOKENS * TOPK, dtype=jnp.int32))
    return owner_table.reshape(EXPERTS, SLOTS)

def dion_step(gradient, moment, factor):
    highest = lax.Precision.HIGHEST
    buffer = moment.astype(jnp.float32) + gradient
    projected = jnp.dot(factor.astype(jnp.float32), buffer.T.astype(jnp.float32), precision=highest, preferred_element_type=jnp.float32)
    gram_matrix = jnp.dot(projected.astype(jnp.float32), projected.T.astype(jnp.float32), precision=highest, preferred_element_type=jnp.float32)
    cholesky_factor = jnp.linalg.cholesky(gram_matrix)
    left_factor = jax.scipy.linalg.solve_triangular(cholesky_factor, projected, lower=True)
    raw_right = jnp.dot(left_factor.astype(jnp.float32), buffer.astype(jnp.float32), precision=highest, preferred_element_type=jnp.float32)
    update = jnp.dot(left_factor.T.astype(jnp.float32), raw_right.astype(jnp.float32), precision=highest, preferred_element_type=jnp.float32)
    new_momentum = (buffer - (1.0 - momentum_decay) * update).astype(jnp.bfloat16)
    column_norm = jnp.sqrt(lax.optimization_barrier(jnp.sum(raw_right * raw_right, axis=1, keepdims=True)) + epsilon)
    return (new_momentum, left_factor, raw_right / column_norm)

def reference(grad_out, routing, gates, hidden, momentum, right_factor):
    owner_table = slot_table(routing)
    flat_gates = gates.reshape(-1)

    def per_expert(operands):
        rows_id, hidden_rows, moment, factor = operands
        is_valid = rows_id >= 0
        safe_index = jnp.where(is_valid, rows_id, 0).astype(jnp.int32)
        token_index = (safe_index // TOPK).astype(jnp.int32)
        scaled = grad_out[token_index].astype(jnp.float32) * flat_gates[safe_index][:, None]
        scaled = jnp.where(is_valid[:, None], scaled, 0.0).astype(jnp.bfloat16)
        gradient = jnp.dot(scaled.T.astype(jnp.float32), hidden_rows.astype(jnp.float32), preferred_element_type=jnp.float32)
        return dion_step(gradient, moment, factor)
    new_momentum, left_factor, new_right = lax.map(per_expert, (owner_table, hidden, momentum, right_factor))
    return (new_momentum, left_factor, new_right)
```

```python
import functools

import functools

import jax
import jax.numpy as jnp
from jax import lax
from jax.experimental import pallas as pl
from jax.experimental.pallas import tpu as pltpu
from jax.sharding import PartitionSpec as P

momentum_decay = 0.95
epsilon = 1e-06
HIGHEST = lax.Precision.HIGHEST
f32 = jnp.float32
bf16 = jnp.bfloat16
CHUNKS = ((0, 1, -1), (2, -2, 3, -3, 4))
META = 16


def ring(size, step):
    return [(i, (i + step) % size) for i in range(size)]


def thirds(x):
    high = x.astype(bf16)
    rest = x - high.astype(f32)
    middle = rest.astype(bf16)
    return high, middle, (rest - middle.astype(f32)).astype(bf16)


def call(kernel, out_shape, cost, **more):
    flops, moved = cost
    return pl.pallas_call(
        kernel,
        grid=(1,),
        out_shape=out_shape,
        compiler_params=pltpu.CompilerParams(vmem_limit_bytes=20 * 1024 * 1024),
        cost_estimate=pl.CostEstimate(flops=flops, bytes_accessed=moved, transcendentals=0),
        **more,
    )


def whole(shape):
    return pl.BlockSpec(shape, lambda i: (0,) * len(shape))


def of_expert(j, shape):
    return pl.BlockSpec((None,) + tuple(shape), lambda i: (j,) + (0,) * len(shape))


def rows_of(ref):
    members, steps, capacity, width = ref.shape
    return ref[...].reshape(members * steps * capacity, width)


def project_kernel(chunks, weights_ref, old_ref, *refs):
    arrived, out_ref = refs[:chunks], refs[-1]
    rank = old_ref.shape[0]
    stacked = jnp.concatenate(thirds(weights_ref[...]), axis=0)
    total = old_ref[...]
    at = 0
    for ref in arrived:
        block = rows_of(ref)
        slots = block.shape[0]
        sums = jnp.dot(stacked[:, at : at + slots], block, preferred_element_type=f32)
        total = total + (sums[:rank] + (sums[rank : 2 * rank] + sums[2 * rank :]))
        at += slots
    out_ref[...] = total


def gradient_kernel(chunks, count, *refs):
    arrived, refs = [rows_of(ref) for ref in refs[:chunks]], refs[chunks:]
    for hidden_ref, out_ref in zip(refs[:count], refs[-count:]):
        total = None
        at = 0
        for block in arrived:
            slots = block.shape[0]
            product = lax.dot_general(
                block,
                hidden_ref[at : at + slots],
                (((0,), (0,)), ((), ())),
                preferred_element_type=f32,
            )
            total = product if total is None else total + product
            at += slots
        out_ref[...] = total.astype(bf16)


def right_kernel(me_ref, left_ref, momentum_ref, *refs):
    grads, out_ref = refs[:-1], refs[-1]
    quarters, rank, width = left_ref.shape
    total = jnp.zeros(out_ref.shape, f32)
    for d, grad_ref in enumerate(grads):
        at = lax.rem(me_ref[0] + d, quarters)
        stacked = jnp.concatenate(thirds(left_ref[at]), axis=0)
        sums = jnp.dot(stacked, momentum_ref[at], preferred_element_type=f32) + jnp.dot(
            stacked, grad_ref[...], preferred_element_type=f32
        )
        total = total + (sums[:rank] + (sums[rank : 2 * rank] + sums[2 * rank :]))
    out_ref[...] = total


def update_kernel(me_ref, left_ref, raw_ref, momentum_ref, *refs):
    out_ref = refs[-1]
    quarters = left_ref.shape[0]
    raw_high, raw_low, _ = thirds((1.0 - momentum_decay) * raw_ref[...])
    raw = jnp.concatenate([raw_high, raw_low, raw_high], axis=0)
    for d in range(quarters):
        at = lax.rem(me_ref[0] + d, quarters)
        high, low, _ = thirds(left_ref[at])
        left = jnp.concatenate([high, high, low], axis=0)
        update = lax.dot_general(
            left, raw, (((0,), (0,)), ((), ())), preferred_element_type=f32
        )
        buffer = momentum_ref[at].astype(f32) + refs[d][...].astype(f32)
        out_ref[at] = (buffer - update).astype(bf16)


def passing_kernel(*refs):
    pass


def passing(values, awaited):
    anywhere = pl.BlockSpec(memory_space=pl.ANY)
    return pl.pallas_call(
        passing_kernel,
        out_shape=[jax.ShapeDtypeStruct(value.shape, value.dtype) for value in values],
        in_specs=[anywhere] * (len(values) + len(awaited)),
        out_specs=[anywhere] * len(values),
        input_output_aliases={i: i for i in range(len(values))},
        cost_estimate=pl.CostEstimate(flops=0, bytes_accessed=0, transcendentals=0),
    )(*values, *awaited)


def pack_kernel(tokens_ref, routing_ref, gates_ref, out_ref):
    rows = tokens_ref.shape[0]
    high, middle, low = (part.astype(f32) for part in thirds(gates_ref[...]))
    out_ref[:rows] = tokens_ref[...]
    out_ref[rows:] = jnp.zeros((META, out_ref.shape[1]), bf16)
    first = jnp.concatenate([routing_ref[...].astype(f32), high], axis=0)
    out_ref[rows:, 0:rows] = first.astype(bf16)
    out_ref[rows:, rows : 2 * rows] = jnp.concatenate([middle, low], axis=0).astype(bf16)


def order_kernel(place_ref, hidden_ref, right_ref, *outs):
    local, along_x, along_z, cores, capacity, cols = hidden_ref.shape
    for j in range(local):
        at = 0
        for steps in CHUNKS:
            for x in range(along_x):
                for c in range(cores):
                    for k in steps:
                        z = lax.rem(place_ref[0] - k + along_z, along_z)
                        outs[j][at : at + capacity] = hidden_ref[j, x, z, c]
                        at += capacity
        outs[j][at:] = jnp.concatenate(thirds(right_ref[j]), axis=0)


def old_kernel(right_ref, momentum_ref, out_ref):
    local, rank = right_ref.shape[:2]
    for j in range(local):
        stacked = jnp.concatenate(thirds(right_ref[j]), axis=0)
        sums = lax.dot_general(
            stacked, momentum_ref[j], (((1,), (1,)), ((), ())), preferred_element_type=f32
        )
        out_ref[j] = sums[:rank] + (sums[rank : 2 * rank] + sums[2 * rank :])


def factor_kernel(me_ref, *refs):
    parts, out_ref = refs[:-1], refs[-1]
    quarters, rank, width = out_ref.shape
    gram = jnp.zeros((rank, rank), f32)
    for ref in parts:
        gram = gram + lax.dot_general(
            ref[...], ref[...], (((1,), (1,)), ((), ())), precision=HIGHEST, preferred_element_type=f32
        )
    row = lax.broadcasted_iota(jnp.int32, (rank, rank), 0)
    column = lax.broadcasted_iota(jnp.int32, (rank, rank), 1)
    below = lax.broadcasted_iota(jnp.int32, (rank, 1), 0)
    table = jnp.concatenate([gram, (row == column).astype(f32)], axis=1)
    scale = jnp.zeros((rank, 1), f32)
    for k in range(rank):
        pivot = table[k : k + 1, k : k + 1]
        scale = jnp.where(below == k, lax.rsqrt(pivot), scale)
        if k + 1 < rank:
            ratio = jnp.where(below > k, table[:, k : k + 1] / pivot, 0.0)
            table = table - ratio * table[k : k + 1, :]
    inverse = scale * table[:, rank:]
    for d, ref in enumerate(parts):
        at = lax.rem(me_ref[0] - d + quarters, quarters)
        out_ref[at] = jnp.dot(inverse, ref[...], precision=HIGHEST, preferred_element_type=f32)


def weigh_kernel(count, *refs):
    out_ref = refs[-1]
    rank, slots = out_ref.shape
    total = jnp.zeros(out_ref.shape, f32)
    for ref in refs[:count]:
        sums = lax.dot_general(
            ref[slots:], ref[:slots], (((1,), (1,)), ((), ())), preferred_element_type=f32
        )
        total = total + (sums[:rank] + (sums[rank : 2 * rank] + sums[2 * rank :]))
    out_ref[...] = total


def slots_kernel(parts, chosen_experts, local, place_ref, *refs):
    out_ref = refs[-1]
    targets, count, _, capacity, width = out_ref.shape
    rows = 128
    pairs = count * targets
    number = lax.broadcasted_iota(jnp.int32, (pairs, 1), 0)
    member = number % targets
    expert = (
        chosen_experts[0] + number // targets
        + local * (member % 2)
        + 2 * local * place_ref[0]
        + 2 * local * 8 * (member // 2)
    ).astype(f32)
    earlier = (
        lax.broadcasted_iota(jnp.int32, (rows, rows), 0)
        < lax.broadcasted_iota(jnp.int32, (rows, rows), 1)
    ).astype(f32).astype(bf16)
    slot = lax.broadcasted_iota(jnp.int32, (pairs, capacity, rows), 1).astype(f32)
    at = 0
    for n, pieces in enumerate(parts):
        block = refs[at][...]
        if pieces > 1:
            block = jnp.concatenate([refs[at + i][...] for i in range(pieces)], axis=0)
        at += pieces
        first = block[rows:, 0:rows].astype(f32)
        second = block[rows:, rows : 2 * rows].astype(f32)
        gates = first[8:] + (second[:8] + second[8:])
        chosen = jnp.zeros((pairs, rows), f32)
        gate_of = jnp.zeros((pairs, rows), f32)
        for k in range(8):
            match = first[k : k + 1] == expert
            chosen = jnp.where(match, 1.0, chosen)
            gate_of = jnp.where(match, gates[k : k + 1], gate_of)
        rank = jnp.dot(chosen.astype(bf16), earlier, preferred_element_type=f32)
        place = jnp.where(chosen > 0.0, rank, -1.0)
        picked = place[:, None, :] == slot
        row_gate = jnp.sum(jnp.where(picked, gate_of[:, None, :], 0.0), axis=2, keepdims=True)
        flat = jnp.where(picked, 1.0, 0.0).reshape(pairs * capacity, rows).astype(bf16)
        values = jnp.dot(flat, block[:rows], preferred_element_type=f32)
        scaled = (values * row_gate.reshape(pairs * capacity, 1)).astype(bf16)
        for j in range(count):
            for target in range(targets):
                start = (j * targets + target) * capacity
                out_ref[target, j, n] = scaled[start : start + capacity]


def body(grad_out, routing, gates, hidden, momentum, right_factor):
    local, slot_count, cols = hidden.shape
    owners = lax.axis_size("expert")
    quarters = lax.axis_size("et")
    me = lax.axis_index("et")
    capacity = slot_count // owners
    rows, width = grad_out.shape
    depth = momentum.shape[1]
    rank = right_factor.shape[1]
    along_x, along_z, cores = 4, 8, 2
    members = along_x * cores
    scalar = me.astype(jnp.int32).reshape(1)
    z_place = (lax.axis_index("expert") // cores % along_z).astype(jnp.int32).reshape(1)
    blocks_of = momentum.reshape(local, quarters, width, cols)
    smem = pl.BlockSpec(memory_space=pltpu.SMEM)

    def device(x, z, c):
        return (x * along_z + z % along_z) * cores + c

    def z_shift(value, step):
        return lax.ppermute(
            value,
            "expert",
            [
                (device(x, z, c), device(x, z + step, c))
                for x in range(along_x)
                for z in range(along_z)
                for c in range(cores)
            ],
        )

    planes = [
        [device(x, z, c) for x in range(along_x) for c in range(cores)] for z in range(along_z)
    ]

    packed = call(
        pack_kernel,
        jax.ShapeDtypeStruct((rows + META, width), bf16),
        (0, 4 * rows * width),
    )(grad_out, routing.T, gates.T)
    ordered = call(
        order_kernel,
        [jax.ShapeDtypeStruct((slot_count + 3 * rank, cols), bf16)] * local,
        (0, 4 * local * slot_count * cols),
        in_specs=[
            smem,
            whole((local, along_x, along_z, cores, capacity, cols)),
            whole(right_factor.shape),
        ],
        out_specs=[whole((slot_count + 3 * rank, cols))] * local,
    )(z_place, hidden.reshape(local, along_x, along_z, cores, capacity, cols), right_factor)
    held = [
        [ordered[j]] + [lax.ppermute(ordered[j], "et", ring(quarters, d)) for d in range(1, quarters)]
        for j in range(local)
    ]
    old = call(
        old_kernel,
        jax.ShapeDtypeStruct((local, rank, depth), f32),
        (6 * local * rank * cols * depth, 2 * local * depth * cols),
    )(right_factor, momentum)
    partial = old
    old = lax.psum_scatter(partial, "et", scatter_dimension=2, tiled=True)

    blocks = {0: [packed]}
    up = down = packed
    first, last = held
    gates_at = {1: first[1::2], 2: last[1::2], 3: first[2:3]}
    for k in range(1, along_z // 2):
        up, down = z_shift(up, 1), z_shift(down, -1)
        blocks[k], blocks[-k] = [up], [down]
        if k in gates_at:
            up, down = passing((up, down), gates_at[k])
    half = 80
    blocks[along_z // 2] = [z_shift(up[:half], 1), z_shift(down[half:], -1)]

    plan = [(CHUNKS[0], tuple(range(local)), [partial])]
    plan += [(CHUNKS[1], (0,), []), (CHUNKS[1], (1,), [old])]
    arrivals = [[] for _ in range(local)]
    sent = ordered[0]
    for steps, chosen, awaited in plan:
        awaited = awaited + [sent]
        parts = tuple(len(blocks[k]) for k in steps)
        operands = [piece for k in steps for piece in blocks[k]]
        shape = (members, len(chosen), len(steps), capacity, width)
        slots = len(chosen) * members * capacity * len(steps)
        sent = call(
            functools.partial(slots_kernel, parts, chosen, local),
            jax.ShapeDtypeStruct(shape, bf16),
            (2 * slots * rows * width, 2 * slots * width),
            in_specs=[smem]
            + [whole(piece.shape) for piece in operands]
            + [pl.BlockSpec(memory_space=pl.ANY)] * len(awaited),
            out_specs=whole(shape),
        )(z_place, *operands, *awaited)
        got = lax.all_to_all(sent, "expert", 0, 0, axis_index_groups=planes, tiled=True)
        for at, j in enumerate(chosen):
            spec = pl.BlockSpec(
                (members, None) + shape[2:], lambda i, at=at: (0, at, 0, 0, 0)
            )
            arrivals[j].append((got, spec))

    new_momentum = None
    ahead, sent = [], []
    anywhere = pl.BlockSpec(memory_space=pl.ANY)
    lefts, raws = [], []
    for j in range(local):
        arrived = [part for part, _ in arrivals[j]]
        specs = [spec for _, spec in arrivals[j]]
        held_specs = [whole(ordered[j].shape)] * quarters
        weights = call(
            functools.partial(weigh_kernel, quarters),
            jax.ShapeDtypeStruct((rank, slot_count), f32),
            (6 * rank * slot_count * cols * quarters, 2 * slot_count * cols * quarters),
            in_specs=held_specs + [anywhere] * len(ahead),
            out_specs=whole((rank, slot_count)),
        )(*held[j], *ahead)
        part = call(
            functools.partial(project_kernel, len(CHUNKS)),
            jax.ShapeDtypeStruct((rank, width), f32),
            (6 * rank * slot_count * width, 2 * slot_count * width),
            in_specs=[whole((rank, slot_count)), of_expert(j, (rank, width))]
            + specs
            + [anywhere] * len(lefts),
            out_specs=whole((rank, width)),
        )(weights, old, *arrived, *lefts)
        moved = [part] + [lax.ppermute(part, "et", ring(quarters, d)) for d in range(1, quarters)]
        grads = call(
            functools.partial(gradient_kernel, len(CHUNKS), quarters),
            [jax.ShapeDtypeStruct((width, cols), bf16)] * quarters,
            (2 * slot_count * width * cols * quarters, 2 * 3 * slot_count * width),
            in_specs=specs + held_specs + [anywhere] * (1 + (len(sent) or 1)),
            out_specs=[whole((width, cols))] * quarters,
        )(*arrived, *held[j], part, *(last[2:3] if j == 0 else sent))
        grads = grads[:1] + passing(grads[1:], moved[1:])
        ahead = grads[:1]
        sent = [grads[0]] + [
            lax.ppermute(grads[d], "et", ring(quarters, quarters - d)) for d in range(1, quarters)
        ]
        left = call(
            factor_kernel,
            jax.ShapeDtypeStruct((quarters, rank, width), f32),
            (12 * rank * rank * depth, 8 * rank * depth),
            in_specs=[smem] + [whole((rank, width))] * quarters,
            out_specs=whole((quarters, rank, width)),
        )(scalar, *moved)
        raw = call(
            right_kernel,
            jax.ShapeDtypeStruct((rank, cols), f32),
            (12 * rank * depth * cols, 4 * depth * cols),
            in_specs=[smem, whole(left.shape), of_expert(j, (quarters, width, cols))]
            + [whole((width, cols))] * quarters,
            out_specs=whole((rank, cols)),
        )(scalar, left, blocks_of, *sent)
        earlier = [] if new_momentum is None else [new_momentum]
        new_momentum = call(
            update_kernel,
            jax.ShapeDtypeStruct(blocks_of.shape, bf16),
            (6 * rank * depth * cols, 6 * depth * cols),
            in_specs=[smem, whole(left.shape), whole(raw.shape), of_expert(j, (quarters, width, cols))]
            + [whole((width, cols))] * quarters
            + [pl.BlockSpec(memory_space=pl.ANY)] * len(earlier),
            out_specs=of_expert(j, (quarters, width, cols)),
            input_output_aliases={4 + quarters: 0} if earlier else {},
        )(scalar, left, raw, blocks_of, *sent, *earlier)
        lefts.append(left)
        raws.append(raw)
    raw = jnp.stack(raws)
    own = jnp.sum(raw * raw, axis=2, keepdims=True)
    sums = own
    for d in range(1, quarters):
        sums = sums + lax.ppermute(own, "et", ring(quarters, d))
    new_right = raw / jnp.sqrt(sums + epsilon)
    left_factor = jnp.stack(lefts).transpose(0, 2, 1, 3).reshape(local, rank, depth)
    return (new_momentum.reshape(momentum.shape), left_factor, new_right)


def solution(mesh):
    placed = (
        P("expert", "et"),
        P("expert", None),
        P("expert", None),
        P("expert", None, "et"),
        P("expert", None, "et"),
        P("expert", None, "et"),
    )
    return jax.shard_map(
        body,
        mesh=mesh,
        in_specs=placed,
        out_specs=(P("expert", None, "et"), P("expert", None, None), P("expert", None, "et")),
        check_vma=False,
    )
```

```python
import functools

import functools

import jax
import jax.numpy as jnp
from jax import lax
from jax.experimental import pallas as pl
from jax.experimental.pallas import tpu as pltpu
from jax.sharding import PartitionSpec as P

momentum_decay = 0.95
epsilon = 1e-06
HIGHEST = lax.Precision.HIGHEST
f32 = jnp.float32
bf16 = jnp.bfloat16
CHUNKS = ((0, 1, -1), (2, -2, 3, -3, 4))
META = 16


def ring(size, step):
    return [(i, (i + step) % size) for i in range(size)]


def thirds(x):
    high = x.astype(bf16)
    rest = x - high.astype(f32)
    middle = rest.astype(bf16)
    return high, middle, (rest - middle.astype(f32)).astype(bf16)


def call(kernel, out_shape, cost, **more):
    flops, moved = cost
    return pl.pallas_call(
        kernel,
        grid=(1,),
        out_shape=out_shape,
        compiler_params=pltpu.CompilerParams(vmem_limit_bytes=20 * 1024 * 1024),
        cost_estimate=pl.CostEstimate(flops=flops, bytes_accessed=moved, transcendentals=0),
        **more,
    )


def whole(shape):
    return pl.BlockSpec(shape, lambda i: (0,) * len(shape))


def of_expert(j, shape):
    return pl.BlockSpec((None,) + tuple(shape), lambda i: (j,) + (0,) * len(shape))


def rows_of(ref):
    members, steps, capacity, width = ref.shape
    return ref[...].reshape(members * steps * capacity, width)


def project_kernel(chunks, weights_ref, old_ref, *refs):
    arrived, out_ref = refs[:chunks], refs[-1]
    rank = old_ref.shape[0]
    stacked = jnp.concatenate(thirds(weights_ref[...]), axis=0)
    total = old_ref[...]
    at = 0
    for ref in arrived:
        block = rows_of(ref)
        slots = block.shape[0]
        sums = jnp.dot(stacked[:, at : at + slots], block, preferred_element_type=f32)
        total = total + (sums[:rank] + (sums[rank : 2 * rank] + sums[2 * rank :]))
        at += slots
    out_ref[...] = total


def gradient_kernel(chunks, count, *refs):
    arrived, refs = [rows_of(ref) for ref in refs[:chunks]], refs[chunks:]
    for hidden_ref, out_ref in zip(refs[:count], refs[-count:]):
        total = None
        at = 0
        for block in arrived:
            slots = block.shape[0]
            product = lax.dot_general(
                block,
                hidden_ref[at : at + slots],
                (((0,), (0,)), ((), ())),
                preferred_element_type=f32,
            )
            total = product if total is None else total + product
            at += slots
        out_ref[...] = total.astype(bf16)


def right_kernel(me_ref, left_ref, momentum_ref, *refs):
    grads, out_ref = refs[:-1], refs[-1]
    quarters, rank, width = left_ref.shape
    total = jnp.zeros(out_ref.shape, f32)
    for d, grad_ref in enumerate(grads):
        at = lax.rem(me_ref[0] + d, quarters)
        stacked = jnp.concatenate(thirds(left_ref[at]), axis=0)
        sums = jnp.dot(stacked, momentum_ref[at], preferred_element_type=f32) + jnp.dot(
            stacked, grad_ref[...], preferred_element_type=f32
        )
        total = total + (sums[:rank] + (sums[rank : 2 * rank] + sums[2 * rank :]))
    out_ref[...] = total


def update_kernel(me_ref, left_ref, raw_ref, momentum_ref, *refs):
    out_ref = refs[-1]
    quarters = left_ref.shape[0]
    raw_high, raw_low, _ = thirds((1.0 - momentum_decay) * raw_ref[...])
    raw = jnp.concatenate([raw_high, raw_low, raw_high], axis=0)
    for d in range(quarters):
        at = lax.rem(me_ref[0] + d, quarters)
        high, low, _ = thirds(left_ref[at])
        left = jnp.concatenate([high, high, low], axis=0)
        update = lax.dot_general(
            left, raw, (((0,), (0,)), ((), ())), preferred_element_type=f32
        )
        buffer = momentum_ref[at].astype(f32) + refs[d][...].astype(f32)
        out_ref[at] = (buffer - update).astype(bf16)


def passing_kernel(*refs):
    pass


def passing(values, awaited):
    anywhere = pl.BlockSpec(memory_space=pl.ANY)
    return pl.pallas_call(
        passing_kernel,
        out_shape=[jax.ShapeDtypeStruct(value.shape, value.dtype) for value in values],
        in_specs=[anywhere] * (len(values) + len(awaited)),
        out_specs=[anywhere] * len(values),
        input_output_aliases={i: i for i in range(len(values))},
        cost_estimate=pl.CostEstimate(flops=0, bytes_accessed=0, transcendentals=0),
    )(*values, *awaited)


def pack_kernel(tokens_ref, routing_ref, gates_ref, out_ref):
    rows = tokens_ref.shape[0]
    high, middle, low = (part.astype(f32) for part in thirds(gates_ref[...]))
    out_ref[:rows] = tokens_ref[...]
    out_ref[rows:] = jnp.zeros((META, out_ref.shape[1]), bf16)
    first = jnp.concatenate([routing_ref[...].astype(f32), high], axis=0)
    out_ref[rows:, 0:rows] = first.astype(bf16)
    out_ref[rows:, rows : 2 * rows] = jnp.concatenate([middle, low], axis=0).astype(bf16)


def order_kernel(place_ref, hidden_ref, right_ref, *outs):
    local, along_x, along_z, cores, capacity, cols = hidden_ref.shape
    for j in range(local):
        at = 0
        for steps in CHUNKS:
            for x in range(along_x):
                for c in range(cores):
                    for k in steps:
                        z = lax.rem(place_ref[0] - k + along_z, along_z)
                        outs[j][at : at + capacity] = hidden_ref[j, x, z, c]
                        at += capacity
        outs[j][at:] = jnp.concatenate(thirds(right_ref[j]), axis=0)


def old_kernel(right_ref, momentum_ref, out_ref):
    local, rank = right_ref.shape[:2]
    for j in range(local):
        stacked = jnp.concatenate(thirds(right_ref[j]), axis=0)
        sums = lax.dot_general(
            stacked, momentum_ref[j], (((1,), (1,)), ((), ())), preferred_element_type=f32
        )
        out_ref[j] = sums[:rank] + (sums[rank : 2 * rank] + sums[2 * rank :])


def factor_kernel(me_ref, *refs):
    parts, out_ref = refs[:-1], refs[-1]
    quarters, rank, width = out_ref.shape
    gram = jnp.zeros((rank, rank), f32)
    for ref in parts:
        gram = gram + lax.dot_general(
            ref[...], ref[...], (((1,), (1,)), ((), ())), precision=HIGHEST, preferred_element_type=f32
        )
    row = lax.broadcasted_iota(jnp.int32, (rank, rank), 0)
    column = lax.broadcasted_iota(jnp.int32, (rank, rank), 1)
    below = lax.broadcasted_iota(jnp.int32, (rank, 1), 0)
    table = jnp.concatenate([gram, (row == column).astype(f32)], axis=1)
    scale = jnp.zeros((rank, 1), f32)
    for k in range(rank):
        pivot = table[k : k + 1, k : k + 1]
        scale = jnp.where(below == k, lax.rsqrt(pivot), scale)
        if k + 1 < rank:
            ratio = jnp.where(below > k, table[:, k : k + 1] / pivot, 0.0)
            table = table - ratio * table[k : k + 1, :]
    inverse = scale * table[:, rank:]
    for d, ref in enumerate(parts):
        at = lax.rem(me_ref[0] - d + quarters, quarters)
        out_ref[at] = jnp.dot(inverse, ref[...], precision=HIGHEST, preferred_element_type=f32)


def weigh_kernel(count, *refs):
    out_ref = refs[-1]
    rank, slots = out_ref.shape
    total = jnp.zeros(out_ref.shape, f32)
    for ref in refs[:count]:
        sums = lax.dot_general(
            ref[slots:], ref[:slots], (((1,), (1,)), ((), ())), preferred_element_type=f32
        )
        total = total + (sums[:rank] + (sums[rank : 2 * rank] + sums[2 * rank :]))
    out_ref[...] = total


def slots_kernel(parts, chosen_experts, local, place_ref, *refs):
    out_ref = refs[-1]
    targets, count, _, capacity, width = out_ref.shape
    rows = 128
    pairs = count * targets
    number = lax.broadcasted_iota(jnp.int32, (pairs, 1), 0)
    member = number % targets
    expert = (
        chosen_experts[0] + number // targets
        + local * (member % 2)
        + 2 * local * place_ref[0]
        + 2 * local * 8 * (member // 2)
    ).astype(f32)
    earlier = (
        lax.broadcasted_iota(jnp.int32, (rows, rows), 0)
        < lax.broadcasted_iota(jnp.int32, (rows, rows), 1)
    ).astype(f32).astype(bf16)
    slot = lax.broadcasted_iota(jnp.int32, (pairs, capacity, rows), 1).astype(f32)
    at = 0
    for n, pieces in enumerate(parts):
        block = refs[at][...]
        if pieces > 1:
            block = jnp.concatenate([refs[at + i][...] for i in range(pieces)], axis=0)
        at += pieces
        first = block[rows:, 0:rows].astype(f32)
        second = block[rows:, rows : 2 * rows].astype(f32)
        gates = first[8:] + (second[:8] + second[8:])
        chosen = jnp.zeros((pairs, rows), f32)
        gate_of = jnp.zeros((pairs, rows), f32)
        for k in range(8):
            match = first[k : k + 1] == expert
            chosen = jnp.where(match, 1.0, chosen)
            gate_of = jnp.where(match, gates[k : k + 1], gate_of)
        rank = jnp.dot(chosen.astype(bf16), earlier, preferred_element_type=f32)
        place = jnp.where(chosen > 0.0, rank, -1.0)
        picked = place[:, None, :] == slot
        row_gate = jnp.sum(jnp.where(picked, gate_of[:, None, :], 0.0), axis=2, keepdims=True)
        flat = jnp.where(picked, 1.0, 0.0).reshape(pairs * capacity, rows).astype(bf16)
        values = jnp.dot(flat, block[:rows], preferred_element_type=f32)
        scaled = (values * row_gate.reshape(pairs * capacity, 1)).astype(bf16)
        for j in range(count):
            for target in range(targets):
                start = (j * targets + target) * capacity
                out_ref[target, j, n] = scaled[start : start + capacity]


def body(grad_out, routing, gates, hidden, momentum, right_factor):
    local, slot_count, cols = hidden.shape
    owners = lax.axis_size("expert")
    quarters = lax.axis_size("et")
    me = lax.axis_index("et")
    capacity = slot_count // owners
    rows, width = grad_out.shape
    depth = momentum.shape[1]
    rank = right_factor.shape[1]
    along_x, along_z, cores = 4, 8, 2
    members = along_x * cores
    scalar = me.astype(jnp.int32).reshape(1)
    z_place = (lax.axis_index("expert") // cores % along_z).astype(jnp.int32).reshape(1)
    blocks_of = momentum.reshape(local, quarters, width, cols)
    smem = pl.BlockSpec(memory_space=pltpu.SMEM)

    def device(x, z, c):
        return (x * along_z + z % along_z) * cores + c

    def z_shift(value, step):
        return lax.ppermute(
            value,
            "expert",
            [
                (device(x, z, c), device(x, z + step, c))
                for x in range(along_x)
                for z in range(along_z)
                for c in range(cores)
            ],
        )

    planes = [
        [device(x, z, c) for x in range(along_x) for c in range(cores)] for z in range(along_z)
    ]

    packed = call(
        pack_kernel,
        jax.ShapeDtypeStruct((rows + META, width), bf16),
        (0, 4 * rows * width),
    )(grad_out, routing.T, gates.T)
    ordered = call(
        order_kernel,
        [jax.ShapeDtypeStruct((slot_count + 3 * rank, cols), bf16)] * local,
        (0, 4 * local * slot_count * cols),
        in_specs=[
            smem,
            whole((local, along_x, along_z, cores, capacity, cols)),
            whole(right_factor.shape),
        ],
        out_specs=[whole((slot_count + 3 * rank, cols))] * local,
    )(z_place, hidden.reshape(local, along_x, along_z, cores, capacity, cols), right_factor)
    held = [
        [ordered[j]] + [lax.ppermute(ordered[j], "et", ring(quarters, d)) for d in range(1, quarters)]
        for j in range(local)
    ]
    old = call(
        old_kernel,
        jax.ShapeDtypeStruct((local, rank, depth), f32),
        (6 * local * rank * cols * depth, 2 * local * depth * cols),
    )(right_factor, momentum)
    partial = old
    old = lax.psum_scatter(partial, "et", scatter_dimension=2, tiled=True)

    blocks = {0: [packed]}
    up = down = packed
    first, last = held
    gates_at = {1: first[1::2], 3: last[1::2]}
    for k in range(1, along_z // 2):
        up, down = z_shift(up, 1), z_shift(down, -1)
        blocks[k], blocks[-k] = [up], [down]
        if k in gates_at:
            up, down = passing((up, down), gates_at[k])
    half = 80
    blocks[along_z // 2] = [z_shift(up[:half], 1), z_shift(down[half:], -1)]

    weights = [
        call(
            functools.partial(weigh_kernel, quarters),
            jax.ShapeDtypeStruct((rank, slot_count), f32),
            (6 * rank * slot_count * cols * quarters, 2 * slot_count * cols * quarters),
        )(*held[j])
        for j in range(local)
    ]
    plan = [(CHUNKS[0], tuple(range(local)), [partial])]
    plan += [(CHUNKS[1], (0,), first[2:3])]
    plan += [(CHUNKS[1], (1,), [old, weights[0]])]
    arrivals = [[] for _ in range(local)]
    sent = ordered[0]
    for steps, chosen, awaited in plan:
        awaited = awaited + [sent]
        parts = tuple(len(blocks[k]) for k in steps)
        operands = [piece for k in steps for piece in blocks[k]]
        shape = (members, len(chosen), len(steps), capacity, width)
        slots = len(chosen) * members * capacity * len(steps)
        sent = call(
            functools.partial(slots_kernel, parts, chosen, local),
            jax.ShapeDtypeStruct(shape, bf16),
            (2 * slots * rows * width, 2 * slots * width),
            in_specs=[smem]
            + [whole(piece.shape) for piece in operands]
            + [pl.BlockSpec(memory_space=pl.ANY)] * len(awaited),
            out_specs=whole(shape),
        )(z_place, *operands, *awaited)
        got = lax.all_to_all(sent, "expert", 0, 0, axis_index_groups=planes, tiled=True)
        for at, j in enumerate(chosen):
            spec = pl.BlockSpec(
                (members, None) + shape[2:], lambda i, at=at: (0, at, 0, 0, 0)
            )
            arrivals[j].append((got, spec))

    new_momentum = None
    sent, ahead = [], []
    anywhere = pl.BlockSpec(memory_space=pl.ANY)
    lefts, raws = [], []
    for j in range(local):
        arrived = [part for part, _ in arrivals[j]]
        specs = [spec for _, spec in arrivals[j]]
        held_specs = [whole(ordered[j].shape)] * quarters
        part = call(
            functools.partial(project_kernel, len(CHUNKS)),
            jax.ShapeDtypeStruct((rank, width), f32),
            (6 * rank * slot_count * width, 2 * slot_count * width),
            in_specs=[whole((rank, slot_count)), of_expert(j, (rank, width))]
            + specs
            + [anywhere] * len(ahead),
            out_specs=whole((rank, width)),
        )(weights[j], old, *arrived, *ahead)
        moved = [part] + [lax.ppermute(part, "et", ring(quarters, d)) for d in range(1, quarters)]
        grads = call(
            functools.partial(gradient_kernel, len(CHUNKS), quarters),
            [jax.ShapeDtypeStruct((width, cols), bf16)] * quarters,
            (2 * slot_count * width * cols * quarters, 2 * 3 * slot_count * width),
            in_specs=specs + held_specs + [anywhere] * (2 if j == 0 else 1),
            out_specs=[whole((width, cols))] * quarters,
        )(*arrived, *held[j], part, *(last[2:3] if j == 0 else []))
        grads = grads[:1] + passing(grads[1:], moved[1:] + sent[1:])
        ahead = moved[1:]
        sent = [grads[0]] + [
            lax.ppermute(grads[d], "et", ring(quarters, quarters - d)) for d in range(1, quarters)
        ]
        left = call(
            factor_kernel,
            jax.ShapeDtypeStruct((quarters, rank, width), f32),
            (12 * rank * rank * depth, 8 * rank * depth),
            in_specs=[smem] + [whole((rank, width))] * quarters,
            out_specs=whole((quarters, rank, width)),
        )(scalar, *moved)
        raw = call(
            right_kernel,
            jax.ShapeDtypeStruct((rank, cols), f32),
            (12 * rank * depth * cols, 4 * depth * cols),
            in_specs=[smem, whole(left.shape), of_expert(j, (quarters, width, cols))]
            + [whole((width, cols))] * quarters,
            out_specs=whole((rank, cols)),
        )(scalar, left, blocks_of, *sent)
        earlier = [] if new_momentum is None else [new_momentum]
        new_momentum = call(
            update_kernel,
            jax.ShapeDtypeStruct(blocks_of.shape, bf16),
            (6 * rank * depth * cols, 6 * depth * cols),
            in_specs=[smem, whole(left.shape), whole(raw.shape), of_expert(j, (quarters, width, cols))]
            + [whole((width, cols))] * quarters
            + [pl.BlockSpec(memory_space=pl.ANY)] * len(earlier),
            out_specs=of_expert(j, (quarters, width, cols)),
            input_output_aliases={4 + quarters: 0} if earlier else {},
        )(scalar, left, raw, blocks_of, *sent, *earlier)
        lefts.append(left)
        raws.append(raw)
    raw = jnp.stack(raws)
    own = jnp.sum(raw * raw, axis=2, keepdims=True)
    sums = own
    for d in range(1, quarters):
        sums = sums + lax.ppermute(own, "et", ring(quarters, d))
    new_right = raw / jnp.sqrt(sums + epsilon)
    left_factor = jnp.stack(lefts).transpose(0, 2, 1, 3).reshape(local, rank, depth)
    return (new_momentum.reshape(momentum.shape), left_factor, new_right)


def solution(mesh):
    placed = (
        P("expert", "et"),
        P("expert", None),
        P("expert", None),
        P("expert", None, "et"),
        P("expert", None, "et"),
        P("expert", None, "et"),
    )
    return jax.shard_map(
        body,
        mesh=mesh,
        in_specs=placed,
        out_specs=(P("expert", None, "et"), P("expert", None, None), P("expert", None, "et")),
        check_vma=False,
    )
```

```python
import functools

import functools

import jax
import jax.numpy as jnp
from jax import lax
from jax.experimental import pallas as pl
from jax.experimental.pallas import tpu as pltpu
from jax.sharding import PartitionSpec as P

momentum_decay = 0.95
epsilon = 1e-06
HIGHEST = lax.Precision.HIGHEST
f32 = jnp.float32
bf16 = jnp.bfloat16
CHUNKS = ((0, 1, -1), (2, -2, 3, -3, 4))
META = 16


def ring(size, step):
    return [(i, (i + step) % size) for i in range(size)]


def thirds(x):
    high = x.astype(bf16)
    rest = x - high.astype(f32)
    middle = rest.astype(bf16)
    return high, middle, (rest - middle.astype(f32)).astype(bf16)


def call(kernel, out_shape, cost, **more):
    flops, moved = cost
    return pl.pallas_call(
        kernel,
        grid=(1,),
        out_shape=out_shape,
        compiler_params=pltpu.CompilerParams(vmem_limit_bytes=20 * 1024 * 1024),
        cost_estimate=pl.CostEstimate(flops=flops, bytes_accessed=moved, transcendentals=0),
        **more,
    )


def whole(shape):
    return pl.BlockSpec(shape, lambda i: (0,) * len(shape))


def of_expert(j, shape):
    return pl.BlockSpec((None,) + tuple(shape), lambda i: (j,) + (0,) * len(shape))


def rows_of(ref):
    members, steps, capacity, width = ref.shape
    return ref[...].reshape(members * steps * capacity, width)


def project_kernel(chunks, weights_ref, old_ref, *refs):
    arrived, out_ref = refs[:chunks], refs[-1]
    rank = old_ref.shape[0]
    stacked = jnp.concatenate(thirds(weights_ref[...]), axis=0)
    total = old_ref[...]
    at = 0
    for ref in arrived:
        block = rows_of(ref)
        slots = block.shape[0]
        sums = jnp.dot(stacked[:, at : at + slots], block, preferred_element_type=f32)
        total = total + (sums[:rank] + (sums[rank : 2 * rank] + sums[2 * rank :]))
        at += slots
    out_ref[...] = total


def gradient_kernel(chunks, count, *refs):
    arrived, refs = [rows_of(ref) for ref in refs[:chunks]], refs[chunks:]
    for hidden_ref, out_ref in zip(refs[:count], refs[-count:]):
        total = None
        at = 0
        for block in arrived:
            slots = block.shape[0]
            product = lax.dot_general(
                block,
                hidden_ref[at : at + slots],
                (((0,), (0,)), ((), ())),
                preferred_element_type=f32,
            )
            total = product if total is None else total + product
            at += slots
        out_ref[...] = total.astype(bf16)


def right_kernel(me_ref, left_ref, momentum_ref, *refs):
    grads, out_ref = refs[:-1], refs[-1]
    quarters, rank, width = left_ref.shape
    total = jnp.zeros(out_ref.shape, f32)
    for d, grad_ref in enumerate(grads):
        at = lax.rem(me_ref[0] + d, quarters)
        stacked = jnp.concatenate(thirds(left_ref[at]), axis=0)
        sums = jnp.dot(stacked, momentum_ref[at], preferred_element_type=f32) + jnp.dot(
            stacked, grad_ref[...], preferred_element_type=f32
        )
        total = total + (sums[:rank] + (sums[rank : 2 * rank] + sums[2 * rank :]))
    out_ref[...] = total


def update_kernel(me_ref, left_ref, raw_ref, momentum_ref, *refs):
    out_ref = refs[-1]
    quarters = left_ref.shape[0]
    raw_high, raw_low, _ = thirds((1.0 - momentum_decay) * raw_ref[...])
    raw = jnp.concatenate([raw_high, raw_low, raw_high], axis=0)
    for d in range(quarters):
        at = lax.rem(me_ref[0] + d, quarters)
        high, low, _ = thirds(left_ref[at])
        left = jnp.concatenate([high, high, low], axis=0)
        update = lax.dot_general(
            left, raw, (((0,), (0,)), ((), ())), preferred_element_type=f32
        )
        buffer = momentum_ref[at].astype(f32) + refs[d][...].astype(f32)
        out_ref[at] = (buffer - update).astype(bf16)


def passing_kernel(*refs):
    pass


def passing(values, awaited):
    anywhere = pl.BlockSpec(memory_space=pl.ANY)
    return pl.pallas_call(
        passing_kernel,
        out_shape=[jax.ShapeDtypeStruct(value.shape, value.dtype) for value in values],
        in_specs=[anywhere] * (len(values) + len(awaited)),
        out_specs=[anywhere] * len(values),
        input_output_aliases={i: i for i in range(len(values))},
        cost_estimate=pl.CostEstimate(flops=0, bytes_accessed=0, transcendentals=0),
    )(*values, *awaited)


def halves_kernel(up_ref, down_ref, *refs):
    upper_ref, lower_ref = refs[-2:]
    upper_ref[...] = up_ref[: upper_ref.shape[0]]
    lower_ref[...] = down_ref[upper_ref.shape[0] :]


def pack_kernel(tokens_ref, routing_ref, gates_ref, out_ref):
    rows = tokens_ref.shape[0]
    high, middle, low = (part.astype(f32) for part in thirds(gates_ref[...]))
    out_ref[:rows] = tokens_ref[...]
    out_ref[rows:] = jnp.zeros((META, out_ref.shape[1]), bf16)
    first = jnp.concatenate([routing_ref[...].astype(f32), high], axis=0)
    out_ref[rows:, 0:rows] = first.astype(bf16)
    out_ref[rows:, rows : 2 * rows] = jnp.concatenate([middle, low], axis=0).astype(bf16)


def order_kernel(place_ref, hidden_ref, right_ref, *outs):
    local, along_x, along_z, cores, capacity, cols = hidden_ref.shape
    for j in range(local):
        at = 0
        for steps in CHUNKS:
            for x in range(along_x):
                for c in range(cores):
                    for k in steps:
                        z = lax.rem(place_ref[0] - k + along_z, along_z)
                        outs[j][at : at + capacity] = hidden_ref[j, x, z, c]
                        at += capacity
        outs[j][at:] = jnp.concatenate(thirds(right_ref[j]), axis=0)


def old_kernel(right_ref, momentum_ref, out_ref):
    local, rank = right_ref.shape[:2]
    for j in range(local):
        stacked = jnp.concatenate(thirds(right_ref[j]), axis=0)
        sums = lax.dot_general(
            stacked, momentum_ref[j], (((1,), (1,)), ((), ())), preferred_element_type=f32
        )
        out_ref[j] = sums[:rank] + (sums[rank : 2 * rank] + sums[2 * rank :])


def factor_kernel(me_ref, *refs):
    parts, out_ref = refs[:-1], refs[-1]
    quarters, rank, width = out_ref.shape
    gram = jnp.zeros((rank, rank), f32)
    for ref in parts:
        gram = gram + lax.dot_general(
            ref[...], ref[...], (((1,), (1,)), ((), ())), precision=HIGHEST, preferred_element_type=f32
        )
    row = lax.broadcasted_iota(jnp.int32, (rank, rank), 0)
    column = lax.broadcasted_iota(jnp.int32, (rank, rank), 1)
    below = lax.broadcasted_iota(jnp.int32, (rank, 1), 0)
    table = jnp.concatenate([gram, (row == column).astype(f32)], axis=1)
    scale = jnp.zeros((rank, 1), f32)
    for k in range(rank):
        pivot = table[k : k + 1, k : k + 1]
        scale = jnp.where(below == k, lax.rsqrt(pivot), scale)
        if k + 1 < rank:
            ratio = jnp.where(below > k, table[:, k : k + 1] / pivot, 0.0)
            table = table - ratio * table[k : k + 1, :]
    inverse = scale * table[:, rank:]
    for d, ref in enumerate(parts):
        at = lax.rem(me_ref[0] - d + quarters, quarters)
        out_ref[at] = jnp.dot(inverse, ref[...], precision=HIGHEST, preferred_element_type=f32)


def weigh_kernel(count, *refs):
    out_ref = refs[-1]
    rank, slots = out_ref.shape
    total = jnp.zeros(out_ref.shape, f32)
    for ref in refs[:count]:
        sums = lax.dot_general(
            ref[slots:], ref[:slots], (((1,), (1,)), ((), ())), preferred_element_type=f32
        )
        total = total + (sums[:rank] + (sums[rank : 2 * rank] + sums[2 * rank :]))
    out_ref[...] = total


def slots_kernel(parts, chosen_experts, local, place_ref, *refs):
    out_ref = refs[-1]
    targets, count, _, capacity, width = out_ref.shape
    rows = 128
    pairs = count * targets
    number = lax.broadcasted_iota(jnp.int32, (pairs, 1), 0)
    member = number % targets
    expert = (
        chosen_experts[0] + number // targets
        + local * (member % 2)
        + 2 * local * place_ref[0]
        + 2 * local * 8 * (member // 2)
    ).astype(f32)
    earlier = (
        lax.broadcasted_iota(jnp.int32, (rows, rows), 0)
        < lax.broadcasted_iota(jnp.int32, (rows, rows), 1)
    ).astype(f32).astype(bf16)
    slot = lax.broadcasted_iota(jnp.int32, (pairs, capacity, rows), 1).astype(f32)
    at = 0
    for n, pieces in enumerate(parts):
        block = refs[at][...]
        if pieces > 1:
            block = jnp.concatenate([refs[at + i][...] for i in range(pieces)], axis=0)
        at += pieces
        first = block[rows:, 0:rows].astype(f32)
        second = block[rows:, rows : 2 * rows].astype(f32)
        gates = first[8:] + (second[:8] + second[8:])
        chosen = jnp.zeros((pairs, rows), f32)
        gate_of = jnp.zeros((pairs, rows), f32)
        for k in range(8):
            match = first[k : k + 1] == expert
            chosen = jnp.where(match, 1.0, chosen)
            gate_of = jnp.where(match, gates[k : k + 1], gate_of)
        rank = jnp.dot(chosen.astype(bf16), earlier, preferred_element_type=f32)
        place = jnp.where(chosen > 0.0, rank, -1.0)
        picked = place[:, None, :] == slot
        row_gate = jnp.sum(jnp.where(picked, gate_of[:, None, :], 0.0), axis=2, keepdims=True)
        flat = jnp.where(picked, 1.0, 0.0).reshape(pairs * capacity, rows).astype(bf16)
        values = jnp.dot(flat, block[:rows], preferred_element_type=f32)
        scaled = (values * row_gate.reshape(pairs * capacity, 1)).astype(bf16)
        for j in range(count):
            for target in range(targets):
                start = (j * targets + target) * capacity
                out_ref[target, j, n] = scaled[start : start + capacity]


def body(grad_out, routing, gates, hidden, momentum, right_factor):
    local, slot_count, cols = hidden.shape
    owners = lax.axis_size("expert")
    quarters = lax.axis_size("et")
    me = lax.axis_index("et")
    capacity = slot_count // owners
    rows, width = grad_out.shape
    depth = momentum.shape[1]
    rank = right_factor.shape[1]
    along_x, along_z, cores = 4, 8, 2
    members = along_x * cores
    scalar = me.astype(jnp.int32).reshape(1)
    z_place = (lax.axis_index("expert") // cores % along_z).astype(jnp.int32).reshape(1)
    blocks_of = momentum.reshape(local, quarters, width, cols)
    smem = pl.BlockSpec(memory_space=pltpu.SMEM)

    def device(x, z, c):
        return (x * along_z + z % along_z) * cores + c

    def z_shift(value, step):
        return lax.ppermute(
            value,
            "expert",
            [
                (device(x, z, c), device(x, z + step, c))
                for x in range(along_x)
                for z in range(along_z)
                for c in range(cores)
            ],
        )

    planes = [
        [device(x, z, c) for x in range(along_x) for c in range(cores)] for z in range(along_z)
    ]

    packed = call(
        pack_kernel,
        jax.ShapeDtypeStruct((rows + META, width), bf16),
        (0, 4 * rows * width),
    )(grad_out, routing.T, gates.T)
    ordered = call(
        order_kernel,
        [jax.ShapeDtypeStruct((slot_count + 3 * rank, cols), bf16)] * local,
        (0, 4 * local * slot_count * cols),
        in_specs=[
            smem,
            whole((local, along_x, along_z, cores, capacity, cols)),
            whole(right_factor.shape),
        ],
        out_specs=[whole((slot_count + 3 * rank, cols))] * local,
    )(z_place, hidden.reshape(local, along_x, along_z, cores, capacity, cols), right_factor)
    held = [
        [ordered[j]] + [lax.ppermute(ordered[j], "et", ring(quarters, d)) for d in range(1, quarters)]
        for j in range(local)
    ]
    old = call(
        old_kernel,
        jax.ShapeDtypeStruct((local, rank, depth), f32),
        (6 * local * rank * cols * depth, 2 * local * depth * cols),
    )(right_factor, momentum)
    partial = old
    old = lax.psum_scatter(partial, "et", scatter_dimension=2, tiled=True)

    blocks = {0: [packed]}
    up = down = packed
    first, last = held
    gates_at = {1: first[1::2]}
    for k in range(1, along_z // 2):
        up, down = z_shift(up, 1), z_shift(down, -1)
        blocks[k], blocks[-k] = [up], [down]
        if k in gates_at:
            up, down = passing((up, down), gates_at[k])
    half = 80
    upper, lower = call(
        halves_kernel,
        [jax.ShapeDtypeStruct((count, width), bf16) for count in (half, rows + META - half)],
        (0, 4 * rows * width),
        in_specs=[whole(packed.shape)] * 2 + [pl.BlockSpec(memory_space=pl.ANY)] * len(last[1::2]),
        out_specs=[whole((count, width)) for count in (half, rows + META - half)],
    )(up, down, *last[1::2])
    blocks[along_z // 2] = [z_shift(upper, 1), z_shift(lower, -1)]

    weights = [
        call(
            functools.partial(weigh_kernel, quarters),
            jax.ShapeDtypeStruct((rank, slot_count), f32),
            (6 * rank * slot_count * cols * quarters, 2 * slot_count * cols * quarters),
        )(*held[j])
        for j in range(local)
    ]
    plan = [(CHUNKS[0], tuple(range(local)), [partial])]
    plan += [(CHUNKS[1], (0,), [])]
    plan += [(CHUNKS[1], (1,), [old, weights[0]])]
    arrivals = [[] for _ in range(local)]
    sent = ordered[0]
    for steps, chosen, awaited in plan:
        awaited = awaited + [sent]
        parts = tuple(len(blocks[k]) for k in steps)
        operands = [piece for k in steps for piece in blocks[k]]
        shape = (members, len(chosen), len(steps), capacity, width)
        slots = len(chosen) * members * capacity * len(steps)
        sent = call(
            functools.partial(slots_kernel, parts, chosen, local),
            jax.ShapeDtypeStruct(shape, bf16),
            (2 * slots * rows * width, 2 * slots * width),
            in_specs=[smem]
            + [whole(piece.shape) for piece in operands]
            + [pl.BlockSpec(memory_space=pl.ANY)] * len(awaited),
            out_specs=whole(shape),
        )(z_place, *operands, *awaited)
        got = lax.all_to_all(sent, "expert", 0, 0, axis_index_groups=planes, tiled=True)
        for at, j in enumerate(chosen):
            spec = pl.BlockSpec(
                (members, None) + shape[2:], lambda i, at=at: (0, at, 0, 0, 0)
            )
            arrivals[j].append((got, spec))

    new_momentum = None
    sent, ahead = [], []
    anywhere = pl.BlockSpec(memory_space=pl.ANY)
    lefts, raws = [], []
    for j in range(local):
        arrived = [part for part, _ in arrivals[j]]
        specs = [spec for _, spec in arrivals[j]]
        held_specs = [whole(ordered[j].shape)] * quarters
        part = call(
            functools.partial(project_kernel, len(CHUNKS)),
            jax.ShapeDtypeStruct((rank, width), f32),
            (6 * rank * slot_count * width, 2 * slot_count * width),
            in_specs=[whole((rank, slot_count)), of_expert(j, (rank, width))]
            + specs
            + [anywhere] * len(ahead),
            out_specs=whole((rank, width)),
        )(weights[j], old, *arrived, *ahead)
        moved = [part] + [lax.ppermute(part, "et", ring(quarters, d)) for d in range(1, quarters)]
        grads = call(
            functools.partial(gradient_kernel, len(CHUNKS), quarters),
            [jax.ShapeDtypeStruct((width, cols), bf16)] * quarters,
            (2 * slot_count * width * cols * quarters, 2 * 3 * slot_count * width),
            in_specs=specs + held_specs + [anywhere] * (2 if j == 0 else 1),
            out_specs=[whole((width, cols))] * quarters,
        )(*arrived, *held[j], part, *(last[2:3] if j == 0 else []))
        grads = grads[:1] + passing(grads[1:], moved[1:] + sent[1:])
        ahead = moved[1:]
        sent = [grads[0]] + [
            lax.ppermute(grads[d], "et", ring(quarters, quarters - d)) for d in range(1, quarters)
        ]
        left = call(
            factor_kernel,
            jax.ShapeDtypeStruct((quarters, rank, width), f32),
            (12 * rank * rank * depth, 8 * rank * depth),
            in_specs=[smem] + [whole((rank, width))] * quarters,
            out_specs=whole((quarters, rank, width)),
        )(scalar, *moved)
        raw = call(
            right_kernel,
            jax.ShapeDtypeStruct((rank, cols), f32),
            (12 * rank * depth * cols, 4 * depth * cols),
            in_specs=[smem, whole(left.shape), of_expert(j, (quarters, width, cols))]
            + [whole((width, cols))] * quarters,
            out_specs=whole((rank, cols)),
        )(scalar, left, blocks_of, *sent)
        earlier = [] if new_momentum is None else [new_momentum]
        new_momentum = call(
            update_kernel,
            jax.ShapeDtypeStruct(blocks_of.shape, bf16),
            (6 * rank * depth * cols, 6 * depth * cols),
            in_specs=[smem, whole(left.shape), whole(raw.shape), of_expert(j, (quarters, width, cols))]
            + [whole((width, cols))] * quarters
            + [pl.BlockSpec(memory_space=pl.ANY)] * len(earlier),
            out_specs=of_expert(j, (quarters, width, cols)),
            input_output_aliases={4 + quarters: 0} if earlier else {},
        )(scalar, left, raw, blocks_of, *sent, *earlier)
        lefts.append(left)
        raws.append(raw)
    raw = jnp.stack(raws)
    own = jnp.sum(raw * raw, axis=2, keepdims=True)
    sums = own
    for d in range(1, quarters):
        sums = sums + lax.ppermute(own, "et", ring(quarters, d))
    new_right = raw / jnp.sqrt(sums + epsilon)
    left_factor = jnp.stack(lefts).transpose(0, 2, 1, 3).reshape(local, rank, depth)
    return (new_momentum.reshape(momentum.shape), left_factor, new_right)


def solution(mesh):
    placed = (
        P("expert", "et"),
        P("expert", None),
        P("expert", None),
        P("expert", None, "et"),
        P("expert", None, "et"),
        P("expert", None, "et"),
    )
    return jax.shard_map(
        body,
        mesh=mesh,
        in_specs=placed,
        out_specs=(P("expert", None, "et"), P("expert", None, None), P("expert", None, "et")),
        check_vma=False,
    )
```
